32 devices in a mesh: fsdp: 8 (over z, x), seq: 4 (over y, core).
Axes of the slice: x: 2, y: 2, z: 4, core: 2. Of those that a mesh axis runs over, the one named last changes fastest.
Arguments:
- tokens: bfloat16 [24, 580, 768], P('fsdp', 'seq'), may hold values from -6 to 6
- routes: int32 [24, 580, 2], P('fsdp'), may hold values from 0 to 3, all different within a row
- ln1_gain: bfloat16 [768], P(('fsdp', 'seq')), may hold values from 0.5 to 1.5
- ln1_bias: bfloat16 [768], P(('fsdp', 'seq')), may hold values from -3 to 3
- w_qkv: bfloat16 [768, 2304], P(('fsdp', 'seq')), may hold values from -0.3125 to 0.3125
- b_qv: bfloat16 [1536], P(('fsdp', 'seq')), may hold values from -4 to 4
- w_proj: bfloat16 [768, 768], P(('fsdp', 'seq')), may hold values from -0.875 to 0.875
- b_proj: bfloat16 [768], P(('fsdp', 'seq')), may hold values from -4 to 4
- ln2_gain: bfloat16 [768], P(('fsdp', 'seq')), may hold values from 0.5 to 1.5
- ln2_bias: bfloat16 [768], P(('fsdp', 'seq')), may hold values from -3 to 3
- w_router: bfloat16 [768, 4], P(('fsdp', 'seq')), may hold values from -0.15625 to 0.15625
- w_in: bfloat16 [4, 768, 3072], P(None, 'fsdp', 'seq'), may hold values from -0.21875 to 0.21875
- b_in: bfloat16 [12288], P(('fsdp', 'seq')), may hold values from -4 to 4
- w_out: bfloat16 [4, 3072, 768], P(None, 'seq', 'fsdp'), may hold values from -0.3125 to 0.3125
- b_out: bfloat16 [3072], P(('fsdp', 'seq')), may hold values from -1.5 to 1.5
- cotangent: bfloat16 [24, 580, 768], P('fsdp', 'seq'), may hold values from -6 to 6
Outputs:
- mixed: bfloat16 [24, 580, 768], P('fsdp', 'seq')
- grad_tokens: float32 [24, 580, 768], P('fsdp', 'seq')
- grad_ln1_gain: float32 [768], P(('fsdp', 'seq'))
- grad_ln1_bias: float32 [768], P(('fsdp', 'seq'))
- grad_w_qkv: float32 [768, 2304], P(('fsdp', 'seq'))
- grad_b_qv: float32 [1536], P(('fsdp', 'seq'))
- grad_w_proj: float32 [768, 768], P(('fsdp', 'seq'))
- grad_b_proj: float32 [768], P(('fsdp', 'seq'))
- grad_ln2_gain: float32 [768], P(('fsdp', 'seq'))
- grad_ln2_bias: float32 [768], P(('fsdp', 'seq'))
- grad_w_router: float32 [768, 4], P(('fsdp', 'seq'))
- grad_w_in: float32 [4, 768, 3072], P(None, 'fsdp', 'seq')
- grad_b_in: float32 [12288], P(('fsdp', 'seq'))
- grad_w_out: float32 [4, 3072, 768], P(None, 'seq', 'fsdp')
- grad_b_out: float32 [3072], P(('fsdp', 'seq'))
The draws below stay inside these ranges and needn't reach their ends.
Inputs may be any that keep to these rules, and one draw needn't show every extreme that they name: `routes`: the two experts of a token slot differ, and each of the 4 experts is named by some slot.
All inputs are finite; a program needn't handle non-finite values.
Results may differ from the reference program's by a relative error of at most 0.014.
Values may be sent and summed in bfloat16 or wider, within the bound.
A program may use at most 256 MiB of HBM per device.

```python
import math
import jax
import jax.numpy as jnp
from jax import lax

D = 768
HEADS = 12
HEAD = 64
FF = 3072
EXPERTS = 4
SLOTS = 145
IMAGES = 24
TOKENS_IMG = 577
N_SEQ = 4


def block_scale(key, extent, cuts, least, largest):
    level, own = 1.0, jax.random.fold_in(key, 6)
    for position, parts in cuts:
        heights = jnp.exp(jax.random.uniform(jax.random.fold_in(own, position), (parts,), jnp.float32, least / len(cuts), largest / len(cuts)))
        level = level * jnp.repeat(heights, extent[position] // parts).reshape([-1 if axis == position else 1 for axis in range(len(extent))])
    return level


def distinct(key, rows, count, top, lift):
    order = jax.random.permutation(jax.random.fold_in(key, 1), count)
    boost = order
    for power in range(3):
        boost = boost * boost // count
    boost = boost * lift // count
    chance = jax.random.randint(jax.random.fold_in(key, 2), (rows, count), 0, 4096) + boost
    sure = jax.random.permutation(jax.random.fold_in(key, 3), rows)[jnp.arange(count) % rows]
    chance = jnp.where(jnp.arange(rows)[:, None] == sure[None, :], 1 << 14, chance)
    priority = chance * count + jnp.arange(count)
    return lax.top_k(priority.astype(jnp.int32), top)[1].astype(jnp.int32)


def bell_draw(own_key, shape, spread, most, pieces=(), held_as=jnp.bfloat16):
    array = jax.random.normal(own_key, shape, jnp.float32) * spread
    if len(pieces) > 0:
        array = block_scale(own_key, shape, pieces, -0.22, 0.18) * array
    return jnp.clip(array, min=-most, max=most).astype(held_as)


def setup_inputs(seed: int = 0) -> dict:
    keys = jax.random.split(jax.random.key(seed), 17)
    tokens = bell_draw(keys[0], (IMAGES, N_SEQ * SLOTS, D), 1.0, 6.0, ((0, 8), (1, 4)))
    routes = distinct(keys[1], IMAGES * (N_SEQ * SLOTS), EXPERTS, 2, 4096).reshape((IMAGES, N_SEQ * SLOTS, 2))
    ln1_gain = jnp.clip(1.0 + 0.1 * jax.random.normal(keys[2], (D,), jnp.float32), 0.5, 1.5).astype(jnp.bfloat16)
    ln1_bias = bell_draw(keys[3], (D,), 0.2, 3.0, ((0, 32),))
    w_qkv = bell_draw(keys[4], (D, 3 * D), (D // 2) ** -0.5, 0.3125, ((0, 32),))
    b_qv = bell_draw(keys[5], (2 * D,), 0.5, 4.0, ((0, 32),))
    w_proj = bell_draw(keys[6], (D, D), (D // 16) ** -0.5, 0.875, ((0, 32),))
    b_proj = bell_draw(keys[7], (D,), 0.3, 4.0, ((0, 32),))
    ln2_gain = jnp.clip(1.0 + 0.1 * jax.random.normal(keys[8], (D,), jnp.float32), 0.5, 1.5).astype(jnp.bfloat16)
    ln2_bias = bell_draw(keys[9], (D,), 0.2, 3.0, ((0, 32),))
    w_router = bell_draw(keys[10], (D, EXPERTS), (2 * D) ** -0.5, 0.15625, ((0, 32),))
    w_in = bell_draw(keys[11], (EXPERTS, D, FF), D ** -0.5, 0.21875, ((1, 8), (2, 4)))
    b_in = bell_draw(keys[12], (EXPERTS * FF,), 0.3, 4.0, ((0, 32),))
    w_out = bell_draw(keys[13], (EXPERTS, FF, D), (FF // 8) ** -0.5, 0.3125, ((1, 4), (2, 8)))
    b_out = bell_draw(keys[14], (EXPERTS * D,), 0.1, 1.5, ((0, 32),))
    cotangent = bell_draw(keys[15], (IMAGES, N_SEQ * SLOTS, D), 1.0, 6.0, ((0, 8), (1, 4)))
    return dict(tokens=tokens, routes=routes, ln1_gain=ln1_gain, ln1_bias=ln1_bias, w_qkv=w_qkv, b_qv=b_qv, w_proj=w_proj, b_proj=b_proj, ln2_gain=ln2_gain, ln2_bias=ln2_bias, w_router=w_router, w_in=w_in, b_in=b_in, w_out=w_out, b_out=b_out, cotangent=cotangent)


@jax.custom_vjp
def low(v):
    return lax.optimization_barrier(v.astype(jnp.bfloat16)).astype(jnp.float32)

@jax.custom_vjp
def low_back(v):
    return v

def low_keep(v):
    return (low(v), None)

def low_pass(kept, grad):
    return (grad,)

def back_keep(v):
    return (v, None)

def back_low(kept, grad):
    return (low(grad),)
low.defvjp(low_keep, low_pass)
low_back.defvjp(back_keep, back_low)
EPSILON = 1e-06
HIGHEST = lax.Precision.HIGHEST

def real_slots():
    kept_list = [place for place in range(N_SEQ * SLOTS) if place < SLOTS or place % SLOTS < SLOTS - 1]
    return jnp.asarray(kept_list, dtype=jnp.int32)

def norm_rows(values, gain_vector, shift_vector):
    average = lax.optimization_barrier(jnp.mean(values, axis=-1, keepdims=True))
    centred = values - average
    variance = lax.optimization_barrier(jnp.mean(centred * centred, axis=-1, keepdims=True))
    return centred * lax.rsqrt(variance + EPSILON) * gain_vector + shift_vector

def block_forward(param_set, inputs_now, routes_now):
    gain_one, shift_one, qkv_weight, qv_shift, proj_weight, proj_shift, gain_two, shift_two, router_weight, inner_weight, inner_shift, outer_weight, outer_shift = param_set
    images, length, width = inputs_now.shape
    normed_one = low(norm_rows(inputs_now, gain_one, shift_one))
    qkv_bias = jnp.concatenate([qv_shift[:width], jnp.zeros((width,), jnp.float32), qv_shift[width:]])
    qkv = jnp.einsum('btd,de->bte', normed_one, qkv_weight, precision=HIGHEST) + qkv_bias
    qkv = low(low_back(qkv)).reshape(images, length, 3, HEADS, HEAD)
    scores = jnp.einsum('bqhd,bkhd->bhqk', qkv[:, :, 0], qkv[:, :, 1], precision=HIGHEST) * HEAD ** (-0.5)
    scores = low_back(scores)
    probs_low = low(jax.nn.softmax(scores, axis=-1))
    attended = jnp.einsum('bhqk,bkhd->bqhd', probs_low, qkv[:, :, 2], precision=HIGHEST)
    attended = low(low_back(attended.reshape(images, length, width)))
    branch = low_back(jnp.einsum('btd,de->bte', attended, proj_weight, precision=HIGHEST) + proj_shift)
    middle = inputs_now + branch
    normed_two = low(norm_rows(middle, gain_two, shift_two))
    logits = jnp.einsum('btd,de->bte', normed_two, router_weight, precision=HIGHEST)
    router = jax.nn.softmax(logits, axis=-1)
    chosen = jax.nn.one_hot(routes_now, EXPERTS, dtype=jnp.float32)
    gates = low(jnp.einsum('btke,bte->btk', chosen, router, precision=HIGHEST))
    expert_weights = jnp.einsum('btk,btke->bte', gates, chosen, precision=HIGHEST)
    mixed_branch = jnp.zeros_like(middle)
    for expert in range(EXPERTS):
        hidden_pre = jnp.einsum('btd,df->btf', normed_two, inner_weight[expert], precision=HIGHEST) + inner_shift[expert]
        hidden_pre = low_back(hidden_pre)
        hidden_act = low(jax.nn.gelu(hidden_pre, approximate=True))
        expert_out = low_back(jnp.einsum('btf,fd->btd', hidden_act, outer_weight[expert], precision=HIGHEST))
        mixed_branch = mixed_branch + expert_weights[..., expert:expert + 1] * (expert_out + outer_shift[expert])
    return middle + mixed_branch

def reference(tokens, routes, ln1_gain, ln1_bias, w_qkv, b_qv, w_proj, b_proj, ln2_gain, ln2_bias, w_router, w_in, b_in, w_out, b_out, cotangent):
    kept_slots = real_slots()
    param_set = (ln1_gain.astype(jnp.float32), ln1_bias.astype(jnp.float32), w_qkv.astype(jnp.float32), b_qv.astype(jnp.float32), w_proj.astype(jnp.float32), b_proj.astype(jnp.float32), ln2_gain.astype(jnp.float32), ln2_bias.astype(jnp.float32), w_router.astype(jnp.float32), w_in.astype(jnp.float32), b_in.astype(jnp.float32).reshape(EXPERTS, FF), w_out.astype(jnp.float32), b_out.astype(jnp.float32).reshape(EXPERTS, D))
    inputs_all = tokens.astype(jnp.float32)[:, kept_slots]
    routes_all = routes[:, kept_slots]
    grads_all = cotangent.astype(jnp.float32)[:, kept_slots]
    per_step = math.gcd(IMAGES, max(1, 4096 // TOKENS_IMG))
    step_count = IMAGES // per_step

    def split_steps(values):
        return values.reshape((step_count, per_step) + values.shape[1:])

    def one_step(totals, batch_now):
        inputs_now, routes_now, grads_now = batch_now

        def forward_now(params_now, inputs_given):
            return block_forward(params_now, inputs_given, routes_now)
        result, pull_back = jax.vjp(forward_now, param_set, inputs_now)
        param_grads, input_grads = pull_back(grads_now)
        return (jax.tree.map(jnp.add, totals, param_grads), (result, input_grads))
    initial = jax.tree.map(jnp.zeros_like, param_set)
    totals, (results, input_grads) = lax.scan(one_step, initial, (split_steps(inputs_all), split_steps(routes_all), split_steps(grads_all)))
    full_shape = (IMAGES, N_SEQ * SLOTS, D)
    mixed = jnp.zeros(full_shape, jnp.float32).at[:, kept_slots].set(results.reshape(IMAGES, TOKENS_IMG, D)).astype(jnp.bfloat16)
    grad_tokens = jnp.zeros(full_shape, jnp.float32).at[:, kept_slots].set(input_grads.reshape(IMAGES, TOKENS_IMG, D))
    grad_gain_one, grad_shift_one, grad_qkv, grad_qv, grad_proj, grad_proj_shift, grad_gain_two, grad_shift_two, grad_router, grad_inner, grad_inner_shift, grad_outer, grad_outer_shift = totals
    return (mixed, grad_tokens, grad_gain_one, grad_shift_one, grad_qkv, grad_qv, grad_proj, grad_proj_shift, grad_gain_two, grad_shift_two, grad_router, grad_inner, grad_inner_shift.reshape(-1), grad_outer, grad_outer_shift.reshape(-1))
```

```python
from functools import partial

import jax
import jax.numpy as jnp
import numpy as np
from jax import lax
from jax.experimental import pallas as pl
from jax.experimental.pallas import tpu as pltpu
from jax.sharding import PartitionSpec as P

HEAD = 64
EPSILON = 1e-06
HIGHEST = lax.Precision.HIGHEST
BF, F32 = jnp.bfloat16, jnp.float32
MESH = pl.DeviceIdType.MESH
GELU_K = float(np.sqrt(2.0 / np.pi))
GELU_C = 0.044715
VMEM = pl.BlockSpec(memory_space=pltpu.VMEM)
ANY = pl.BlockSpec(memory_space=pl.ANY)
LIMIT = 60 * 2**20


def dot(a, b):
    return lax.dot_general(a, b, (((1,), (0,)), ((), ())), preferred_element_type=F32)


def dot_t(a, b):
    return lax.dot_general(a, b, (((1,), (1,)), ((), ())), preferred_element_type=F32)


def span(start, size):
    return pl.ds(pl.multiple_of(start, 16), size)


class Net:
    def __init__(self, fsdp):
        self.f, self.s = lax.axis_index("fsdp"), lax.axis_index("seq")
        f, s = self.f, self.s
        self.zn = fsdp // 2
        self.z, self.x = f // 2, f % 2
        self.s1 = (s // 2) * 2 + 1 - s % 2
        self.s2 = (1 - s // 2) * 2 + s % 2
        self.s3 = 3 - s
        self.core, self.yp, self.dg = (f, self.s1), (f, self.s2), (f, self.s3)
        self.xp = (self.z * 2 + 1 - self.x, s)
        self.zk = [(self.z + k) % self.zn for k in range(1, self.zn)]
        self.zp = [(zz * 2 + self.x, s) for zz in self.zk]
        self.zsrc = [(self.z + self.zn - k) % self.zn for k in range(1, self.zn)]
        self.seqs = [(self.s1, self.core), (self.s2, self.yp), (self.s3, self.dg)]

    def greet(self):
        barrier = pltpu.get_barrier_semaphore()
        partners = [self.core, self.yp, self.dg, self.xp] + self.zp
        for device in partners:
            pl.semaphore_signal(barrier, inc=1, device_id=device, device_id_type=MESH)
        pl.semaphore_wait(barrier, len(partners))


def rcopy(src, dst, sems, index, device):
    send, recv = sems
    copy = pltpu.make_async_remote_copy(
        src_ref=src,
        dst_ref=dst,
        send_sem=send.at[index],
        recv_sem=recv.at[index],
        device_id=device,
        device_id_type=MESH,
    )
    copy.start()
    return copy


def lcopy(src, dst, sem):
    copy = pltpu.make_async_copy(src, dst, sem)
    copy.start()
    return copy


def norm_parts(values):
    centred = values - jnp.mean(values, axis=-1, keepdims=True)
    scale = lax.rsqrt(jnp.mean(centred * centred, axis=-1, keepdims=True) + EPSILON)
    return centred * scale, scale


def lanes(rows):
    return lax.broadcasted_iota(jnp.int32, (rows, 128), 1)


def half_masks():
    lane = lanes(1)
    low = jnp.where(lane < HEAD, 1.0, 0.0).astype(BF)
    return low, jnp.where(lane < HEAD, 0.0, 1.0).astype(BF)


def soft_columns(scores):
    weights = jnp.exp(scores - jnp.max(scores, axis=0, keepdims=True))
    return weights * (1.0 / jnp.sum(weights, axis=0, keepdims=True))


def forward_kernel(
    dims,
    x_own, wq_own, wp_own, mask, key_bias, pick, place, c_own, win_own, wout_own,
    h1, qkv, att, h2, mid, gate, router, w6, wp, sm, c_img, w_in, w_out,
    x_img, qs, wps, w32, p32, sm32, wr, vt, *sems,
):
    fsdp, images, sp, experts, shard = dims
    net = Net(fsdp)
    f, s, z, x = net.f, net.s, net.z, net.x
    img = 4 * sp
    rowblock = w_in.shape[1] // fsdp
    (a2a, tok, cot, qg, qf, pg, pf, ps, wg, wf, at) = zip(sems[0:22:2], sems[1:22:2])
    local = sems[22]
    open_copies = []

    def go(*args):
        copy = rcopy(*args)
        open_copies.append(copy)
        return copy

    def own_rows(i, who):
        return span(img * i + sp * who, sp)

    net.greet()
    first = [go(wq_own.at[who], qs.at[f, s], a2a, k, dev) for k, (who, dev) in enumerate(net.seqs)]
    keep = [lcopy(wq_own.at[s], qs.at[f, s], local.at[0]), lcopy(wp_own, wps.at[s, f], local.at[1])]
    toks, cots = [], []
    for i in range(images):
        keep.append(lcopy(x_own.at[i], x_img.at[own_rows(i, s)], local.at[2 + i]))
        toks.append([go(x_own.at[i], x_img.at[own_rows(i, s)], tok, k * images + i, dev) for k, dev in enumerate((net.core, net.yp))])
    for c in first:
        c.wait_recv()
    keep[0].wait()
    q_z = [go(qs.at[f], qs.at[f], qg, k + 1, dev) for k, dev in enumerate(net.zp)]
    q_x = [go(qs.at[f], qs.at[f], qg, 0, net.xp)]
    keep[1].wait()
    p_z = [go(wps.at[s, f], wps.at[s, f], pg, k + 1, dev) for k, dev in enumerate(net.zp)]
    p_x = [go(wps.at[s, f], wps.at[s, f], pg, 0, net.xp)]
    pieces = 2 * experts
    own = [(win_own, wout_own)[p % 2].at[p // 2] for p in range(pieces)]
    whole = [(w_in, w_out)[p % 2].at[p // 2] for p in range(pieces)]

    def rows_of(p, who):
        return whole[p].at[span(rowblock * who, rowblock)]

    w_z, w_x = [None] * pieces, [None] * pieces

    def send_z(p):
        w_z[p] = [go(own[p], rows_of(p, f), wg, p * fsdp + k + 1, dev) for k, dev in enumerate(net.zp)]

    def send_x(p):
        w_x[p] = [go(own[p], rows_of(p, f), wg, p * fsdp, net.xp)]
        keep.append(lcopy(own[p], rows_of(p, f), local.at[2 + 2 * images + p]))

    def pump(p):
        for k, zz in enumerate(net.zsrc):
            w_z[p][k].wait_recv()
            block = rows_of(p, zz * 2 + x)
            w_x[p].append(go(block, block, wf, p * fsdp + k, net.xp))

    send_z(0)
    send_z(1)
    for i in range(images):
        toks[i][1].wait_recv()
        rows = own_rows(i, net.s2)
        toks[i].append(go(x_img.at[rows], x_img.at[rows], tok, 2 * images + i, net.core))
    for k, zz in enumerate(net.zsrc):
        q_z[k].wait_recv()
        q_x.append(go(qs.at[zz * 2 + x], qs.at[zz * 2 + x], qf, k, net.xp))
    for k, zz in enumerate(net.zsrc):
        p_z[k].wait_recv()
        block = wps.at[s, zz * 2 + x]
        p_x.append(go(block, block, pf, k, net.xp))
    for p in range(pieces):
        send_x(p)
        if p > 1:
            send_z(p)
    for i in range(images):
        cots.append([go(c_own.at[i], c_img.at[own_rows(i, s)], cot, k * images + i, dev) for k, dev in enumerate((net.core, net.yp))])
        keep.append(lcopy(c_own.at[i], c_img.at[own_rows(i, s)], local.at[2 + images + i]))
    for c in q_x:
        c.wait_recv()

    low, high = half_masks()
    qk_width = w32.shape[1]

    def unpack(d, carry):
        block = qs[d // 4, d % 4].astype(F32)
        w32[pl.ds(pl.multiple_of(shard * d, 8), shard), :] = block[:shard]
        sm32[d] = block[shard:]
        return carry

    lax.fori_loop(0, 4 * fsdp, unpack, 0)
    w6[:, 0:384] = w32[:, 0:384].astype(BF)
    third = w32[:, 384:512]
    w6[:, 384:512] = third.astype(BF) * low
    w6[:, 512:640] = pltpu.roll(third, HEAD, 1).astype(BF) * low
    w6[:, 640:768] = w32[:, 512:640].astype(BF)
    width = w6.shape[0]
    devices = 4 * fsdp
    device = lax.broadcasted_iota(jnp.int32, (devices, width), 0)

    def expand(row, lane, picker, places):
        spread = dot(sm32[:, row, lane : lane + 128].astype(BF), pick[picker])
        return jnp.where(device == places, spread, 0.0)

    for r in range(5):
        sm[r : r + 1, :] = jnp.sum(expand(0, 128 * r, 0, place[0:1, :]), axis=0, keepdims=True)
    sm[5:6, :] = jnp.sum(expand(1, 0, 1, place[1:2, :] + 4 * s), axis=0, keepdims=True)
    spread_out = dot(sm32[:, 1, 128:256].astype(BF), pick[2])
    per_expert = devices // experts
    wr[...] = jnp.zeros(wr.shape, BF)
    for e in range(experts):
        sm[8 + e : 9 + e, :] = jnp.sum(
            jnp.where(device == place[2:3, :] + per_expert * e, spread_out, 0.0), axis=0, keepdims=True
        )
        half = width // 2
        for j in range(2):
            sm[12 + e : 13 + e, half * j : half * (j + 1)] = sm32[per_expert * e + 2 * s + j, 1:2, 256 : 256 + half]
        sm[16 + e : 17 + e, :] = jnp.sum(expand(2, 128 * e, 0, place[0:1, :]), axis=0, keepdims=True)
    wr[0:8, :] = jnp.concatenate([sm[16:20, :], jnp.zeros((4, width), F32)], axis=0).astype(BF)

    scale_row = jnp.where(lax.broadcasted_iota(jnp.int32, (1, width), 1) % 384 < 128, HEAD**-0.5, 1.0)
    gain_one, shift_one = sm[0:1, :], sm[1:2, :]

    for c in keep[2 : 2 + images]:
        c.wait()
    for i in range(images):
        toks[i][0].wait_recv()
        toks[i][2].wait_recv()

        def first_norm(j, carry):
            rows = span(img * i + sp * j, sp)
            normed, _ = norm_parts(x_img[rows, :].astype(F32))
            h1[rows, :] = (normed * gain_one + shift_one).astype(BF)
            return carry

        lax.fori_loop(0, 4, first_norm, 0)
        here = pl.ds(img * i, img)
        for n in range(3):
            cols = slice(256 * n, 256 * n + 256)
            part = dot(h1[here, :], w6[:, cols]) + sm[5:6, cols]
            qkv[here, cols] = (part * scale_row[:, cols]).astype(BF)
    pump(0)

    def attend(i):
        base = img * i
        here = pl.ds(base, img)
        vt[0] = qkv[here, 256:384].astype(F32).T.astype(BF)
        vt[1] = qkv[here, 640:768].astype(F32).T.astype(BF)

        def chunk(c, carry):
            rows = span(base + 128 * c, 128)
            q01, q2 = qkv[rows, 0:128], qkv[rows, 384:512]
            outs = []
            for q, cols, t in ((q01 * low, 128, 0), (q01 * high, 128, 0), (q2, 512, 1)):
                scores = dot_t(qkv[here, cols : cols + 128], q) + key_bias[...]
                outs.append(dot(vt[t], soft_columns(scores).astype(BF)))
            both = jnp.concatenate([outs[0][:HEAD], outs[1][HEAD:]], axis=0)
            att[s, rows, 0:128] = both.T.astype(BF)
            att[s, rows, 128:256] = outs[2].T.astype(BF)
            return carry

        lax.fori_loop(0, img // 128, chunk, 0)

    att_sent = []
    for i in range(images):
        attend(i)
        rows = pl.ds(img * i, img)
        att_sent.append([go(att.at[s, rows], att.at[s, rows], at, k * images + i, dev) for k, dev in enumerate((net.core, net.yp))])
        if i > 0:
            att_sent[i - 1][1].wait_recv()
            rows = pl.ds(img * (i - 1), img)
            att_sent[i - 1].append(go(att.at[net.s2, rows], att.at[net.s2, rows], at, 2 * images + i - 1, net.core))
        pump(i + 1)
    p_rows = pl.ds(0, fsdp)
    for c in p_x:
        c.wait_recv()
    block = wps.at[s, p_rows]
    p_seq = [go(wps.at[s], wps.at[s], ps, k, dev) for k, dev in enumerate((net.core, net.yp))]
    p_seq[1].wait_recv()
    p_seq.append(go(wps.at[net.s2], wps.at[net.s2], ps, 2, net.core))
    att_sent[-1][1].wait_recv()
    rows = pl.ds(img * (images - 1), img)
    att_sent[-1].append(go(att.at[net.s2, rows], att.at[net.s2, rows], at, 3 * images - 1, net.core))
    p_seq[0].wait_recv()
    p_seq[2].wait_recv()

    def unpack_proj(d, carry):
        p32[pl.ds(pl.multiple_of(shard * d, 8), shard), :] = wps[d % 4, d // 4].astype(F32)[:shard]
        return carry

    lax.fori_loop(0, 4 * fsdp, unpack_proj, 0)
    wp[...] = p32[...].astype(BF)

    gain_two, shift_two, proj_shift = sm[2:3, :], sm[3:4, :], sm[4:5, :]
    group = width // 4
    tile = img // 2
    for i in range(images):
        att_sent[i][0].wait_recv()
        att_sent[i][2].wait_recv()

        def after(j, carry):
            rows = span(img * i + tile * j, tile)
            total = x_img[rows, :].astype(F32) + proj_shift
            for g in range(4):
                total += dot(att[g, rows, 0:group], wp[group * g : group * (g + 1), :])
            mid[rows, :] = total
            normed, _ = norm_parts(total)
            low_rows = (normed * gain_two + shift_two).astype(BF)
            h2[rows, :] = low_rows
            lane = lanes(tile)
            logits = jnp.where(lane < experts, dot_t(low_rows, wr[...]), -1e30)
            weights = jnp.exp(logits - jnp.max(logits, axis=1, keepdims=True))
            probs = weights * (1.0 / jnp.sum(weights, axis=1, keepdims=True))
            router[rows, :] = probs
            gate[rows, :] = probs.astype(BF).astype(F32) * mask[rows, :]
            return carry

        lax.fori_loop(0, 2, after, 0)
        if images + 1 + i < pieces:
            pump(images + 1 + i)
    for i in range(images):
        cots[i][1].wait_recv()
        rows = own_rows(i, net.s2)
        cots[i].append(go(c_img.at[rows], c_img.at[rows], cot, 2 * images + i, net.core))
    for p in range(2 * images + 1, pieces):
        pump(p)
    for i in range(images):
        cots[i][0].wait_recv()
        cots[i][2].wait_recv()
    for p in range(pieces):
        for c in w_x[p]:
            c.wait_recv()
    for c in open_copies:
        c.wait_send()
    for c in keep[2 + images :]:
        c.wait()


def run_forward(dims, x_own, wq_own, wp_own, mask, key_bias, pick, place, c_own, win_own, wout_own):
    fsdp, images, sp, experts, shard = dims
    rows, width = images * 4 * sp, x_own.shape[-1]
    S = jax.ShapeDtypeStruct
    counts = [3, 3 * images, 3 * images, fsdp, fsdp, fsdp, fsdp, 3, 2 * experts * fsdp, 2 * experts * fsdp, 3 * images]
    sems = [pltpu.SemaphoreType.DMA((n,)) for n in counts for _ in range(2)]
    sems.append(pltpu.SemaphoreType.DMA((2 + 2 * images + 2 * experts,)))
    return pl.pallas_call(
        partial(forward_kernel, dims),
        out_shape=(
            S((rows, width), BF), S((rows, width), BF), S((4, rows, 256), BF), S((rows, width), BF),
            S((rows, width), F32), S((rows, 128), F32), S((rows, 128), F32),
            S((width, width), BF), S((width, width), BF), S((24, width), F32),
            S((rows, width), BF), S((experts, width, win_own.shape[2]), BF), S((experts, width, wout_own.shape[2]), BF),
        ),
        in_specs=[VMEM] * 7 + [ANY] * 3,
        out_specs=[VMEM] * 10 + [ANY] * 3,
        scratch_shapes=[
            pltpu.VMEM((rows, width), BF),
            pltpu.VMEM((fsdp, 4, 32, 640), BF),
            pltpu.VMEM((4, fsdp, 32, width), BF),
            pltpu.VMEM((width, 640), F32),
            pltpu.VMEM((width, width), F32),
            pltpu.VMEM((4 * fsdp, 8, 640), F32),
            pltpu.VMEM((128, width), BF),
            pltpu.VMEM((2, 128, 4 * sp), BF),
        ] + sems,
        compiler_params=pltpu.CompilerParams(collective_id=0, has_side_effects=True, vmem_limit_bytes=LIMIT),
    )(x_own, wq_own, wp_own, mask, key_bias, pick, place, c_own, win_own, wout_own)


def pack_rows(values, sp):
    return jnp.pad(values, ((0, 0), (0, sp - values.shape[1]), (0, 0)))


def prepare(t):
    fsdp, seqs = lax.axis_size("fsdp"), lax.axis_size("seq")
    s = lax.axis_index("seq")
    images, slots, width = t["tokens"].shape
    experts = t["w_in"].shape[0]
    sp = (slots + 15) // 16 * 16
    shard = t["w_qkv"].shape[0]
    dims = (fsdp, images, sp, experts, shard)
    slot = np.arange(slots)
    own_valid = ((s == 0) | (slot < slots - 1))[None, :, None]
    c_own = pack_rows(jnp.where(own_valid, t["cotangent"], jnp.zeros((), BF)), sp)
    x_own = pack_rows(t["tokens"], sp)
    split = t["w_qkv"].reshape(shard, 3, seqs, 192)
    parts = [split[:, n, :, :128] for n in range(3)] + [split[:, n, :, 128:] for n in range(3)]
    cols = jnp.concatenate(parts + [jnp.zeros((shard, seqs, 64), BF)], axis=-1)

    def lane_row(*items):
        placed = []
        for item in items:
            placed.append(jnp.pad(item, (0, -item.shape[0] % 128)))
        row = jnp.concatenate(placed)
        return jnp.pad(row, (0, 640 - row.shape[0]))

    small = jnp.stack(
        [
            lane_row(t["ln1_gain"], t["ln1_bias"], t["ln2_gain"], t["ln2_bias"], t["b_proj"]),
            lane_row(t["b_qv"], t["b_out"], t["b_in"]),
            lane_row(*[t["w_router"][:, e] for e in range(experts)]),
        ]
        + [jnp.zeros((640,), BF)] * 5
    )
    wq_own = jnp.concatenate([jnp.swapaxes(cols, 0, 1), jnp.broadcast_to(small, (seqs, 8, 640))], axis=1)
    wp_own = jnp.pad(t["w_proj"], ((0, 32 - shard), (0, 0)))
    wout_own = jnp.swapaxes(t["w_out"], 1, 2)
    routes = t["routes"].reshape(images, seqs, slots, 2)
    chosen = (routes[..., None] == np.arange(128)).astype(F32).sum(axis=3)
    alive = (np.arange(seqs)[:, None] == 0) | (slot < slots - 1)
    chosen = jnp.where(alive[None, :, :, None], chosen, 0.0)
    mask = jnp.pad(chosen, ((0, 0), (0, 0), (0, sp - slots), (0, 0))).reshape(-1, 128)
    live = np.zeros((seqs, sp), bool)
    live[:, : slots - 1] = True
    live[0, slots - 1] = True
    key_bias = jnp.broadcast_to(jnp.asarray(np.where(live.reshape(-1, 1), 0.0, -1e30), F32), (seqs * sp, 128))
    lane = np.arange(width)
    per = t["b_qv"].shape[0]
    q_lane = np.where(lane % 384 < 128, lane % 384, 0) + np.where(lane >= 384, 128, 0)
    v_lane = np.where(lane % 384 >= 256, lane % 384 - 256, 0) + np.where(lane >= 384, 128, 0)
    is_q, is_v = lane % 384 < 128, lane % 384 >= 256
    live_lane = (is_q | is_v) & ((lane < 384) | (lane % 128 < 64))
    at = np.where(is_q, q_lane, v_lane)
    pick = np.zeros((3, 128, width), np.float32)
    pick[0, lane % shard, lane] = 1
    pick[1, (at % per)[live_lane], lane[live_lane]] = 1
    out_shard = t["b_out"].shape[0]
    pick[2, lane % out_shard, lane] = 1
    place = np.zeros((8, width), np.int32)
    place[0], place[2] = lane // shard, lane // out_shard
    place[1] = at // per + np.where(is_v, width // per, 0)
    return dims, (
        x_own, wq_own, wp_own, mask, key_bias, jnp.asarray(pick, BF), jnp.asarray(place), c_own, t["w_in"], wout_own,
    ), own_valid


def reduce_piece(net, go, p, grads, halves, arrived, xs, zs):
    return go(grads.at[:, 1 - net.x], halves, xs, p, net.xp)


def expert_kernel(
    dims,
    h2, c, gate, b_in, w_in, w_out,
    owned, mixed, bias_grad, halves, quarters,
    win, wout, h2t, ct, dpre, act, mix, back, dots, ring, htmp, qtmp, cs, cr, ys, yr, *sems,
):
    fsdp, images, sp, experts, shard = dims
    net = Net(fsdp)
    f, s, z, x = net.f, net.s, net.z, net.x
    img = 4 * sp
    rows_all, width = h2.shape
    ff = win.shape[1]
    xs, zs, core_sems, y_sems = zip(sems[0:8:2], sems[1:8:2])
    local = sems[8]
    open_copies = []
    pieces = 2 * experts
    slots = ring.shape[0]

    def go(*args):
        copy = rcopy(*args)
        open_copies.append(copy)
        return copy

    def load(e):
        return [lcopy(w_in.at[e], win, local.at[0]), lcopy(w_out.at[e], wout, local.at[1])]

    weights = load(0)
    net.greet()
    mix[...] = jnp.zeros(mix.shape, F32)
    back[...] = jnp.zeros(back.shape, F32)
    dots[...] = jnp.zeros(dots.shape, F32)
    bias_grad[...] = jnp.zeros(bias_grad.shape, F32)

    def turn(j, carry):
        rows = pl.ds(pl.multiple_of(128 * j, 128), 128)
        h2t[:, rows] = h2[rows, :].astype(F32).T.astype(BF)
        ct[:, rows] = c[rows, :].astype(F32).T.astype(BF)
        return carry

    lax.fori_loop(0, rows_all // 128, turn, 0)

    sent_x, sent_z = [None] * pieces, [None] * pieces

    def ship(p):
        sent_x[p] = go(ring.at[p % slots, :, 1 - x], halves.at[p], xs, p, net.xp)

    def relay(p):
        sent_x[p].wait_recv()
        pltpu.sync_copy(halves.at[p], htmp)
        sent_z[p] = []
        for k, zz in enumerate(net.zk):
            mine = ring.at[p % slots, zz, x]
            mine[...] = (mine[...].astype(F32) + htmp[zz].astype(F32)).astype(BF)
            sent_z[p].append(go(mine, quarters.at[p, k], zs, 3 * p + k, net.zp[k]))
        owned[p] = ring[p % slots, z, x].astype(F32) + htmp[z].astype(F32)

    def finish(p):
        for copy in sent_z[p]:
            copy.wait_recv()
        pltpu.sync_copy(quarters.at[p], qtmp)
        owned[p] = owned[p] + qtmp[0].astype(F32) + qtmp[1].astype(F32) + qtmp[2].astype(F32)

    tile = img // 2
    lane = lanes(tile)

    def expert_rows(e, t):
        rows = span(tile * t, tile)
        h_rows, c_rows = h2[rows, :], c[rows, :]
        gates = jnp.sum(jnp.where(lane == e, gate[rows, :], 0.0), axis=1, keepdims=True)
        inner = jnp.zeros((tile, 1), F32)
        for n in range(ff // 256):
            cols = slice(256 * n, 256 * n + 256)
            pre = dot(h_rows, win[:, cols]) + b_in[e : e + 1, cols]
            d_act = dot(c_rows, wout[:, cols])
            square = pre * pre
            half = 0.5 + 0.5 * jnp.tanh(pre * (GELU_K + (GELU_K * GELU_C) * square))
            value = pre * half
            low_value = value.astype(BF).astype(F32)
            slope = half + value * (1.0 - half) * (2 * GELU_K + (6 * GELU_K * GELU_C) * square)
            inner += jnp.sum(low_value * d_act, axis=1, keepdims=True)
            act[rows, cols] = (low_value * gates).astype(BF)
            d_pre = slope * (d_act * gates)
            bias_grad[e : e + 1, cols] += jnp.sum(d_pre, axis=0, keepdims=True)
            dpre[rows, cols] = d_pre.astype(BF)
        dots[rows, :] += jnp.where(lane == e, inner, 0.0)
        for n in range(width // 256):
            cols = slice(256 * n, 256 * n + 256)
            mix[rows, cols] += dot_t(act[rows, :], wout[cols, :])
            back[rows, cols] += dot_t(dpre[rows, :], win[cols, :])

    core_sent, y_sent = [], []

    def pack(i, who):
        rows = span(img * i + sp * who, sp)
        return mix[rows, :], back[rows, :], dots[rows, :]

    def core_send(i):
        for k, who in enumerate((net.s1, net.s3)):
            at = 0
            for part in pack(i, who):
                cs[i, k, :, at : at + part.shape[1]] = part.astype(BF)
                at += part.shape[1]
            core_sent.append(go(cs.at[i, k], cr.at[i, k], core_sems, 2 * i + k, net.core))

    def y_send(i):
        core_sent[2 * i + 1].wait_recv()
        at = 0
        for part in pack(i, net.s2):
            cols = slice(at, at + part.shape[1])
            ys[i, :, cols] = (part + cr[i, 1, :, cols].astype(F32)).astype(BF)
            at += part.shape[1]
        y_sent.append(go(ys.at[i], yr.at[i], y_sems, i, net.yp))

    def collect(i):
        core_sent[2 * i].wait_recv()
        y_sent[i].wait_recv()
        at = 0
        for part in pack(i, s):
            cols = slice(at, at + part.shape[1])
            mixed[i, :, cols] = part + cr[i, 0, :, cols].astype(F32) + yr[i, :, cols].astype(F32)
            at += part.shape[1]

    def grads(e):
        for which, (left, right) in enumerate(((h2t, dpre), (ct, act))):
            p = 2 * e + which
            if p >= slots:
                sent_x[p - slots].wait_send()
                for copy in sent_z[p - slots]:
                    copy.wait_send()
            for n in range(ff // 256):
                cols = slice(256 * n, 256 * n + 256)
                block = dot(left[...], right[:, cols]).astype(BF)
                ring[p % slots, :, :, :, cols] = block.reshape(net.zn, 2, width // fsdp, 256)
            ship(p)

    for e in range(experts):
        for copy in weights:
            copy.wait()
        if e < experts - 1:
            lax.fori_loop(0, 2 * images, lambda t, carry: (expert_rows(e, t), carry)[1], 0)
            weights = load(e + 1)
        else:
            weights = []
            for i in range(images):
                lax.fori_loop(2 * i, 2 * i + 2, lambda t, carry: (expert_rows(e, t), carry)[1], 0)
                core_send(i)
                if i > 0:
                    y_send(i - 1)
            y_send(images - 1)
        if e > 1:
            relay(2 * e - 4)
            relay(2 * e - 3)
        grads(e)
    for i in range(images):
        collect(i)
    for p in range(2 * experts - 4, pieces):
        relay(p)
        finish(p - (2 * experts - 4))
    for p in range(4, pieces):
        finish(p)
    for copy in open_copies:
        if copy not in ():
            pass
    drained = set()
    for p in range(pieces - slots):
        drained.update([id(sent_x[p])] + [id(copy) for copy in sent_z[p]])
    for copy in open_copies:
        if id(copy) not in drained:
            copy.wait_send()


def run_experts(dims, h2, c, gate, b_in, w_in, w_out):
    fsdp, images, sp, experts, shard = dims
    rows, width = h2.shape
    ff = w_in.shape[2]
    block = width // fsdp
    wide = 2 * width + 128
    pieces = 2 * experts
    zn = fsdp // 2
    S = jax.ShapeDtypeStruct
    counts = [pieces, 3 * pieces, 2 * images, images]
    sems = [pltpu.SemaphoreType.DMA((n,)) for n in counts for _ in range(2)]
    sems.append(pltpu.SemaphoreType.DMA((2,)))
    V = pltpu.VMEM
    return pl.pallas_call(
        partial(expert_kernel, dims),
        out_shape=(
            S((pieces, block, ff), F32), S((images, sp, wide), F32), S((8, ff), F32),
            S((pieces, zn, block, ff), BF), S((pieces, zn - 1, block, ff), BF),
        ),
        in_specs=[VMEM] * 4 + [ANY] * 2,
        out_specs=[VMEM] * 3 + [ANY] * 2,
        scratch_shapes=[
            V((width, ff), BF), V((width, ff), BF), V((width, rows), BF), V((width, rows), BF),
            V((rows, ff), BF), V((rows, ff), BF), V((rows, width), F32), V((rows, width), F32), V((rows, 128), F32),
            V((4, zn, 2, block, ff), BF), V((zn, block, ff), BF), V((zn - 1, block, ff), BF),
            V((images, 2, sp, wide), BF), V((images, 2, sp, wide), BF), V((images, sp, wide), BF), V((images, sp, wide), BF),
        ] + sems,
        compiler_params=pltpu.CompilerParams(collective_id=1, has_side_effects=True, vmem_limit_bytes=LIMIT),
    )(h2, c, gate, b_in, w_in, w_out)


def backward_kernel(
    dims,
    wide, sm, key_bias, bias_grad, w6, wp, h1, qkv, x_own, mid, h2, att, c, gate, router, mask,
    mixed, g_tokens, g_qkv, g_proj, small,
    mo, ho, co, ao, gate_o, router_o, mask_o, wr, bo, da, a_img, dmid, db, dl, h1t, dqkv, kt, acc, dh1, cs, cr, ys, yr,
    total_p, total_q, grad_p, grad_q, half_p, half_q, quarter_p, quarter_q, sum_p, sum_q, seq_p, s_sum, s_core, s_y, s_x, s_z, *sems,
):
    fsdp, images, sp, experts, shard = dims
    net = Net(fsdp)
    f, s, z, x = net.f, net.s, net.z, net.x
    img = 4 * sp
    width = w6.shape[0]
    group = width // 4
    a_s, core_s, y_s, x_s, z_s, q_s, small_s = zip(sems[0:14:2], sems[1:14:2])
    local = sems[14]
    open_copies = []

    def go(*args):
        copy = rcopy(*args)
        open_copies.append(copy)
        return copy

    def at_rows(i, who):
        return span(img * i + sp * who, sp)

    own_copies = []
    for n, (src, dst) in enumerate(((mid, mo), (h2, ho), (c, co), (gate, gate_o), (router, router_o), (mask, mask_o))):
        for i in range(images):
            own_copies.append(lcopy(src.at[at_rows(i, s)], dst.at[pl.ds(sp * i, sp)], local.at[n * images + i]))
    for i in range(images):
        own_copies.append(lcopy(att.at[:, at_rows(i, s)], ao.at[:, pl.ds(sp * i, sp)], local.at[6 * images + i]))
    net.greet()
    used = images * sp
    for ref in (ho, co, db):
        ref[used:, :] = jnp.zeros((ref.shape[0] - used, width), BF)
    for ref in (gate_o, dl):
        ref[used:, :] = jnp.zeros((ref.shape[0] - used, 128), F32)
    ao[:, used:, :] = jnp.zeros((4, ao.shape[1] - used, 256), BF)
    da[...] = jnp.zeros(da.shape, BF)
    small[...] = jnp.zeros(small.shape, F32)
    wr[...] = jnp.zeros(wr.shape, BF)
    bo[...] = jnp.zeros(bo.shape, BF)
    wr[0:8, :] = jnp.concatenate([sm[16:20, :], jnp.zeros((4, width), F32)], axis=0).astype(BF)
    bo[0:8, :] = jnp.concatenate([sm[8:12, :], jnp.zeros((4, width), F32)], axis=0).astype(BF)
    for copy in own_copies:
        copy.wait()

    gain_two = sm[2:3, :]
    da_sent = []
    for i in range(images):
        rows = pl.ds(sp * i, sp)
        middle, cc = mo[rows, :], co[rows, :]
        grad32 = cc.astype(F32)
        g = gate_o[rows, :]
        mixed[i] = (middle + wide[i, :, 0:width] + dot(g.astype(BF), bo[...])).astype(BF)
        d_router = (wide[i, :, 2 * width :] + dot_t(cc, bo[...])) * mask_o[rows, :]
        probs = router_o[rows, :]
        d_logits = probs * (d_router - jnp.sum(probs * d_router, axis=1, keepdims=True))
        dl[rows, :] = d_logits
        d_h2 = wide[i, :, width : 2 * width] + dot(d_logits.astype(BF), wr[...])
        normed, scale = norm_parts(middle)
        inner = d_h2 * gain_two
        change = inner - jnp.mean(inner, axis=1, keepdims=True) - normed * jnp.mean(inner * normed, axis=1, keepdims=True)
        d_middle = grad32 + change * scale
        dmid[rows, :] = d_middle
        branch = d_middle.astype(BF)
        db[rows, :] = branch
        small[2:3, :] += jnp.sum(d_h2 * normed, axis=0, keepdims=True)
        small[3:4, :] += jnp.sum(d_h2, axis=0, keepdims=True)
        small[4:5, :] += jnp.sum(branch.astype(F32), axis=0, keepdims=True)
        for j in range(4):
            da[j, rows, 0:group] = dot_t(branch, wp[group * j : group * (j + 1), :]).astype(BF)
        for k, (who, dev) in enumerate(net.seqs):
            da_sent.append(go(da.at[who, rows], a_img.at[at_rows(i, s)], a_s, 3 * i + k, dev))
        a_img[at_rows(i, s), :] = da[s, rows, :]

    small[8:16, :] = jnp.concatenate(
        [dot(gate_o[...].T.astype(BF), co[...])[0:4], dot(dl[...].T.astype(BF), ho[...])[0:4]], axis=0
    )
    for e in range(experts):
        small[pl.ds(16 + 4 * e + s, 1), :] = bias_grad[e : e + 1, :]
    for j in range(4):
        turned = ao[j].astype(F32).T.astype(BF)
        total_p[group * j : group * (j + 1), :] = dot(turned, db[...])[0:group]
    grad_p[...] = total_p[...].astype(BF).reshape(grad_p.shape)
    sent_p = go(grad_p.at[:, 1 - x], half_p, x_s, 0, net.xp)

    def turn(j, carry):
        rows = pl.ds(pl.multiple_of(128 * j, 128), 128)
        h1t[:, rows] = h1[rows, :].astype(F32).T.astype(BF)
        return carry

    lax.fori_loop(0, h1.shape[0] // 128, turn, 0)
    total_q[...] = jnp.zeros(total_q.shape, F32)

    def relay(grad, half, quarter, owned, sent, base):
        sent.wait_recv()
        copies = []
        for k, zz in enumerate(net.zk):
            grad[zz, x] = (grad[zz, x].astype(F32) + half[zz].astype(F32)).astype(BF)
            copies.append(go(grad.at[zz, x], quarter.at[k], z_s, base + k, net.zp[k]))
        owned[...] = grad[z, x].astype(F32) + half[z].astype(F32)
        return copies

    def finish(quarter, owned, copies):
        for copy in copies:
            copy.wait_recv()
        owned[...] += quarter[0].astype(F32) + quarter[1].astype(F32) + quarter[2].astype(F32)

    low, high = half_masks()

    def attend_back(i):
        base = img * i
        here = pl.ds(base, img)
        kt[0] = qkv[here, 128:256].astype(F32).T.astype(BF)
        kt[1] = qkv[here, 512:640].astype(F32).T.astype(BF)
        acc[...] = jnp.zeros(acc.shape, F32)

        def chunk(n, carry):
            rows = span(base + 128 * n, 128)
            q01, q2 = qkv[rows, 0:128], qkv[rows, 384:512]
            a01, a2 = a_img[rows, 0:128], a_img[rows, 128:256]
            outs = []
            for q, a, col, t in ((q01 * low, a01 * low, 128, 0), (q01 * high, a01 * high, 128, 0), (q2, a2, 512, 1)):
                probs = soft_columns(dot_t(qkv[here, col : col + 128], q) + key_bias[...])
                d_probs = dot_t(qkv[here, col + 128 : col + 256], a)
                inner = jnp.sum(probs * d_probs, axis=0, keepdims=True)
                d_scores = (probs * (d_probs - inner)).astype(BF)
                acc[2 * t] += dot(d_scores, q)
                acc[2 * t + 1] += dot(probs.astype(BF), a)
                outs.append(dot(kt[t], d_scores))
            both = jnp.concatenate([outs[0][:HEAD], outs[1][HEAD:]], axis=0)
            local_rows = span(128 * n, 128)
            dqkv[local_rows, 0:128] = (both.T * HEAD**-0.5).astype(BF)
            dqkv[local_rows, 384:512] = (outs[2].T * HEAD**-0.5).astype(BF)
            return carry

        lax.fori_loop(0, img // 128, chunk, 0)
        for n, col in enumerate((128, 256, 512, 640)):
            dqkv[:, col : col + 128] = acc[n].astype(BF)

    core_sent, y_sent = [], []

    def y_send(i):
        core_sent[2 * i + 1].wait_recv()
        ys[i] = (dh1[at_rows(i, net.s2), :] + cr[i, 1].astype(F32)).astype(BF)
        y_sent.append(go(ys.at[i], yr.at[i], y_s, i, net.yp))

    p_z = None
    column_sum = jnp.zeros((1, width), F32)
    for i in range(images):
        for k in range(3):
            da_sent[3 * i + k].wait_recv()
        attend_back(i)
        here = pl.ds(img * i, img)
        for n in range(width // 256):
            cols = slice(256 * n, 256 * n + 256)
            dh1[here, cols] = dot_t(dqkv[...], w6[cols, :])
        for k, who in enumerate((net.s1, net.s3)):
            cs[i, k] = dh1[at_rows(i, who), :].astype(BF)
            core_sent.append(go(cs.at[i, k], cr.at[i, k], core_s, 2 * i + k, net.core))
        column_sum = column_sum + jnp.sum(dqkv[...].astype(F32), axis=0, keepdims=True)
        for n in range(width // 256):
            cols = slice(256 * n, 256 * n + 256)
            total_q[:, cols] += dot(h1t[:, here], dqkv[:, cols])
        if i > 0:
            y_send(i - 1)
        if i == 0:
            p_z = relay(grad_p, half_p, quarter_p, sum_p, sent_p, 0)
    y_send(images - 1)
    small[pl.ds(32 + s, 1), :] = column_sum
    blocks = grad_q.shape[:3]
    grad_q[:, :, :, 0:384] = total_q[:, 0:384].astype(BF).reshape(blocks + (384,))
    third = total_q[:, 384:512] + pltpu.roll(total_q[:, 512:640], HEAD, 1)
    grad_q[:, :, :, 384:512] = third.astype(BF).reshape(blocks + (128,))
    grad_q[:, :, :, 512:640] = total_q[:, 640:768].astype(BF).reshape(blocks + (128,))
    sent_q = go(grad_q.at[:, 1 - x], half_q, x_s, 1, net.xp)
    finish(quarter_p, sum_p, p_z)

    def part_rows(who):
        return pl.ds(pl.multiple_of(shard * who, 8), shard)

    p_seq = [go(sum_p.at[part_rows(who)], seq_p.at[k], q_s, k, dev) for k, (who, dev) in enumerate(net.seqs)]

    gain_one = sm[0:1, :]
    for i in range(images):
        core_sent[2 * i].wait_recv()
        y_sent[i].wait_recv()
        d_h1 = dh1[at_rows(i, s), :] + cr[i, 0].astype(F32) + yr[i].astype(F32)
        normed, scale = norm_parts(x_own[i].astype(F32))
        inner = d_h1 * gain_one
        change = inner - jnp.mean(inner, axis=1, keepdims=True) - normed * jnp.mean(inner * normed, axis=1, keepdims=True)
        g_tokens[i] = dmid[pl.ds(sp * i, sp), :] + change * scale
        small[0:1, :] += jnp.sum(d_h1 * normed, axis=0, keepdims=True)
        small[1:2, :] += jnp.sum(d_h1, axis=0, keepdims=True)

    s_sum[0] = small[...]
    hop = go(s_sum.at[0], s_core, small_s, 0, net.core)
    hop.wait_recv()
    s_sum[1] = s_sum[0] + s_core[...]
    hop = go(s_sum.at[1], s_y, small_s, 1, net.yp)
    q_z = relay(grad_q, half_q, quarter_q, sum_q, sent_q, 3)
    hop.wait_recv()
    s_sum[2] = s_sum[1] + s_y[...]
    hop = go(s_sum.at[2], s_x, small_s, 2, net.xp)
    for copy in p_seq:
        copy.wait_recv()
    g_proj[...] = sum_p[part_rows(s), :] + seq_p[0] + seq_p[1] + seq_p[2]
    hop.wait_recv()
    s_sum[3] = s_sum[2] + s_x[...]
    hops = [go(s_sum.at[3], s_z.at[k], small_s, 3 + k, dev) for k, dev in enumerate(net.zp)]
    finish(quarter_q, sum_q, q_z)
    q_seq = [go(sum_q.at[part_rows(who)], g_qkv.at[s], q_s, 3 + k, dev) for k, (who, dev) in enumerate(net.seqs)]
    g_qkv[s] = sum_q[part_rows(s), :]
    for copy in hops:
        copy.wait_recv()
    small[...] = s_sum[3] + s_z[0] + s_z[1] + s_z[2]
    for copy in q_seq:
        copy.wait_recv()
    for copy in open_copies:
        copy.wait_send()


def run_backward(dims, *operands):
    fsdp, images, sp, experts, shard = dims
    rows, width = images * 4 * sp, operands[4].shape[0]
    zn, block = fsdp // 2, width // fsdp
    own = (images * sp + 127) // 128 * 128
    S, V = jax.ShapeDtypeStruct, pltpu.VMEM
    counts = [3 * images, 2 * images, images, 2, 6, 6, 6]
    sems = [pltpu.SemaphoreType.DMA((n,)) for n in counts for _ in range(2)]
    sems.append(pltpu.SemaphoreType.DMA((7 * images,)))
    return pl.pallas_call(
        partial(backward_kernel, dims),
        out_shape=(
            S((images, sp, width), BF), S((images, sp, width), F32), S((4, shard, 640), F32), S((shard, width), F32), S((40, width), F32),
        ),
        in_specs=[VMEM] * 9 + [ANY] * 7,
        out_specs=[VMEM] * 5,
        scratch_shapes=[
            V((own, width), F32), V((own, width), BF), V((own, width), BF), V((4, own, 256), BF),
            V((own, 128), F32), V((own, 128), F32), V((own, 128), F32), V((128, width), BF), V((128, width), BF),
            V((4, own, 256), BF), V((rows, 256), BF), V((own, width), F32), V((own, width), BF), V((own, 128), F32),
            V((width, rows), BF), V((4 * sp, width), BF), V((2, 128, 4 * sp), BF), V((4, 4 * sp, 128), F32), V((rows, width), F32),
            V((images, 2, sp, width), BF), V((images, 2, sp, width), BF), V((images, sp, width), BF), V((images, sp, width), BF),
            V((width, width), F32), V((width, width), F32),
            V((zn, 2, block, width), BF), V((zn, 2, block, 640), BF), V((zn, block, width), BF), V((zn, block, 640), BF),
            V((zn - 1, block, width), BF), V((zn - 1, block, 640), BF), V((block, width), F32), V((block, 640), F32),
            V((3, shard, width), F32), V((4, 40, width), F32), V((40, width), F32), V((40, width), F32), V((40, width), F32), V((3, 40, width), F32),
        ] + sems,
        compiler_params=pltpu.CompilerParams(collective_id=2, has_side_effects=True, vmem_limit_bytes=LIMIT),
    )(*operands)


def unpack_small(small, t, fsdp, seqs):
    experts, width = t["w_in"].shape[0], t["tokens"].shape[2]
    d = lax.axis_index("fsdp") * seqs + lax.axis_index("seq")

    def piece(flat, size):
        return lax.dynamic_slice_in_dim(flat, d * size, size, 0)

    shard = t["ln1_gain"].shape[0]
    rows = lax.dynamic_slice(small[0:5], (0, d * shard), (5, shard))
    router = lax.dynamic_slice(small[12:16], (0, d * shard), (4, shard)).T
    out_bias = piece(small[8:12].reshape(-1), t["b_out"].shape[0])
    in_bias = piece(small[16:32].reshape(-1), t["b_in"].shape[0])
    tiles = small[32:36]
    q = jnp.concatenate([tiles[:, 0:128], tiles[:, 384:448]], axis=1).reshape(-1)
    v = jnp.concatenate([tiles[:, 256:384], tiles[:, 640:704]], axis=1).reshape(-1)
    qv = piece(jnp.concatenate([q, v]), t["b_qv"].shape[0])
    return rows, router, out_bias, in_bias, qv


NAMES = (
    "tokens", "routes", "ln1_gain", "ln1_bias", "w_qkv", "b_qv", "w_proj", "b_proj", "ln2_gain", "ln2_bias", "w_router",
    "w_in", "b_in", "w_out", "b_out", "cotangent",
)


def per_device(*args):
    t = dict(zip(NAMES, args))
    fsdp, seqs = lax.axis_size("fsdp"), lax.axis_size("seq")
    dims, operands, own_valid = prepare(t)
    _, images, sp, experts, shard = dims
    slots, width = t["tokens"].shape[1:]
    x_own, mask, key_bias = operands[0], operands[3], operands[4]
    h1, qkv, att, h2, mid, gate, router, w6, wp, sm, c_img, w_in, w_out = run_forward(dims, *operands)
    owned, wide, bias_grad, _, _ = run_experts(dims, h2, c_img, gate, sm[12:20], w_in, w_out)
    mixed, g_tokens, g_qkv, g_proj, small = run_backward(
        dims, wide, sm, key_bias, bias_grad, w6, wp, h1, qkv, x_own, mid, h2, att, c_img, gate, router, mask
    )
    rows, router_grad, out_bias, in_bias, qv = unpack_small(small, t, fsdp, seqs)
    cols = jnp.swapaxes(g_qkv, 0, 1)
    parts = [
        jnp.concatenate([cols[:, :, 128 * n : 128 * n + 128], cols[:, :, 384 + 64 * n : 448 + 64 * n]], axis=2).reshape(shard, -1)
        for n in range(3)
    ]
    owned = owned.reshape((experts, 2) + owned.shape[1:])
    return (
        jnp.where(own_valid, mixed[:, :slots], jnp.zeros((), BF)),
        jnp.where(own_valid, g_tokens[:, :slots], 0.0),
        rows[0],
        rows[1],
        jnp.concatenate(parts, axis=1),
        qv,
        g_proj,
        rows[4],
        rows[2],
        rows[3],
        router_grad,
        owned[:, 0],
        in_bias,
        jnp.swapaxes(owned[:, 1], 1, 2),
        out_bias,
    )


def norm_rows(values, gain_vector, shift_vector):
    average = jnp.mean(values, axis=-1, keepdims=True)
    centred = values - average
    variance = jnp.mean(centred * centred, axis=-1, keepdims=True)
    return centred * lax.rsqrt(variance + EPSILON) * gain_vector + shift_vector


def softmax_last(values):
    return jax.nn.softmax(values, axis=-1)


def gelu_tanh(values):
    return jax.nn.gelu(values, approximate=True)


def masked_scores(queries, keys_now, key_valid):
    head_scale = queries.shape[-1] ** (-0.5)
    scores = (
        jnp.einsum("bqhd,bkhd->bhqk", queries, keys_now, preferred_element_type=jnp.float32)
        * head_scale
    )
    return jnp.where(key_valid, scores, -jnp.inf)


def attend_block(key_valid, qkv_block):
    queries = qkv_block[:, :, 0]
    keys_now = qkv_block[:, :, 1]
    values_now = qkv_block[:, :, 2]
    scores = masked_scores(queries, keys_now, key_valid)
    highest = jnp.max(scores, axis=-1, keepdims=True)
    weights = jnp.exp(scores - highest)
    totals = jnp.sum(weights, axis=-1, keepdims=True)
    probs_low = (weights / totals).astype(jnp.bfloat16)
    attended = jnp.einsum(
        "bhqk,bkhd->bqhd", probs_low, values_now, preferred_element_type=jnp.float32
    )
    return (attended.astype(jnp.bfloat16), (highest + jnp.log(totals))[..., 0])


def attend_back(key_valid, pieces):
    qkv_block, grad_block, log_block = pieces
    queries = qkv_block[:, :, 0]
    keys_now = qkv_block[:, :, 1]
    values_now = qkv_block[:, :, 2]
    head_scale = queries.shape[-1] ** (-0.5)
    scores = masked_scores(queries, keys_now, key_valid)
    probs = jnp.exp(scores - log_block[..., None])
    grad_probs = jnp.einsum(
        "bqhd,bkhd->bhqk", grad_block, values_now, preferred_element_type=jnp.float32
    )
    grad_values = jnp.einsum(
        "bhqk,bqhd->bkhd",
        probs.astype(jnp.bfloat16),
        grad_block,
        preferred_element_type=jnp.float32,
    )
    inner = jnp.sum(probs * grad_probs, axis=-1, keepdims=True)
    grad_scores = (probs * (grad_probs - inner)).astype(jnp.bfloat16)
    grad_queries = (
        jnp.einsum("bhqk,bkhd->bqhd", grad_scores, keys_now, preferred_element_type=jnp.float32)
        * head_scale
    )
    grad_keys = (
        jnp.einsum("bhqk,bqhd->bkhd", grad_scores, queries, preferred_element_type=jnp.float32)
        * head_scale
    )
    return jnp.stack([grad_queries, grad_keys, grad_values], axis=2).astype(jnp.bfloat16)


def expert_pass(rows_now, grad_now, inner_now, outer_now, bias_now):
    pre_now = jnp.dot(rows_now, inner_now, preferred_element_type=jnp.float32) + bias_now
    active_now = gelu_tanh(pre_now).astype(jnp.bfloat16)
    result = jnp.einsum("tq,dq->td", active_now, outer_now, preferred_element_type=jnp.float32)
    grad_active = jnp.dot(grad_now, outer_now, preferred_element_type=jnp.float32)
    _, gelu_pull = jax.vjp(gelu_tanh, pre_now)
    grad_pre = gelu_pull(grad_active)[0].astype(jnp.bfloat16)
    inner_grad = jnp.einsum("td,tq->dq", rows_now, grad_pre, preferred_element_type=jnp.float32)
    outer_grad = jnp.einsum("td,tq->dq", grad_now, active_now, preferred_element_type=jnp.float32)
    bias_grad = jnp.sum(grad_pre.astype(jnp.float32), axis=0)
    grad_rows_now = jnp.einsum("tq,dq->td", grad_pre, inner_now, preferred_element_type=jnp.float32)
    return (result, grad_rows_now, inner_grad, outer_grad, bias_grad)


def per_device_general(
    tokens,
    routes,
    ln1_gain,
    ln1_bias,
    w_qkv,
    b_qv,
    w_proj,
    b_proj,
    ln2_gain,
    ln2_bias,
    w_router,
    w_in,
    b_in,
    w_out,
    b_out,
    cotangent,
):
    seq_count = lax.axis_size("seq")
    seq_place = lax.axis_index("seq")
    images, slots, width = tokens.shape
    experts = w_in.shape[0]
    quarter = w_in.shape[2]
    length = seq_count * slots
    head_local = width // HEAD // seq_count
    local_width = head_local * HEAD
    (
        gain_one,
        shift_one,
        qkv_weight,
        qv_shift,
        proj_weight,
        proj_shift,
        gain_two,
        shift_two,
        router_weight,
        inner_shift,
        outer_shift,
    ) = (
        lax.all_gather(ln1_gain, ("fsdp", "seq"), axis=0, tiled=True),
        lax.all_gather(ln1_bias, ("fsdp", "seq"), axis=0, tiled=True),
        lax.all_gather(w_qkv, ("fsdp", "seq"), axis=0, tiled=True),
        lax.all_gather(b_qv, ("fsdp", "seq"), axis=0, tiled=True),
        lax.all_gather(w_proj, ("fsdp", "seq"), axis=0, tiled=True),
        lax.all_gather(b_proj, ("fsdp", "seq"), axis=0, tiled=True),
        lax.all_gather(ln2_gain, ("fsdp", "seq"), axis=0, tiled=True),
        lax.all_gather(ln2_bias, ("fsdp", "seq"), axis=0, tiled=True),
        lax.all_gather(w_router, ("fsdp", "seq"), axis=0, tiled=True),
        lax.all_gather(b_in, ("fsdp", "seq"), axis=0, tiled=True),
        lax.all_gather(b_out, ("fsdp", "seq"), axis=0, tiled=True),
    )
    gain_one = gain_one.astype(jnp.float32)
    shift_one = shift_one.astype(jnp.float32)
    gain_two = gain_two.astype(jnp.float32)
    shift_two = shift_two.astype(jnp.float32)
    slot_index = jnp.arange(slots)
    own_valid = ((seq_place == 0) | (slot_index < slots - 1))[None, :, None]
    places = jnp.arange(length)
    key_valid = (places < slots) | (places % slots < slots - 1)
    inner_all = inner_shift.reshape(experts, -1).astype(jnp.float32)
    outer_bias = outer_shift.reshape(experts, width).astype(jnp.float32)
    outer_local = jnp.swapaxes(w_out, 1, 2)
    inner_bias = lax.dynamic_slice_in_dim(inner_all, seq_place * quarter, quarter, 1)
    inner_weight, outer_weight = (
        lax.all_gather(w_in, "fsdp", axis=1, tiled=True),
        lax.all_gather(outer_local, "fsdp", axis=1, tiled=True),
    )
    inputs32 = tokens.astype(jnp.float32)
    normed_one = norm_rows(inputs32, gain_one, shift_one).astype(jnp.bfloat16)
    qv32 = qv_shift.astype(jnp.float32)
    qkv_bias = jnp.concatenate([qv32[:width], jnp.zeros((width,), jnp.float32), qv32[width:]])
    qkv = (
        jnp.einsum("btd,de->bte", normed_one, qkv_weight, preferred_element_type=jnp.float32)
        + qkv_bias
    )
    qkv_split = qkv.astype(jnp.bfloat16).reshape(images, slots, 3, seq_count, local_width)
    qkv_heads = lax.all_to_all(qkv_split, "seq", split_axis=3, concat_axis=1, tiled=True)
    blocks = qkv_heads.reshape(1, images, length, 3, head_local, HEAD)
    attended_heads, log_totals = lax.map(partial(attend_block, key_valid), blocks)
    attended_back = lax.all_to_all(
        attended_heads.reshape(images, length, 1, local_width),
        "seq",
        split_axis=1,
        concat_axis=2,
        tiled=True,
    )
    attended_tok = attended_back.reshape(images, slots, width)
    branch = jnp.einsum(
        "btd,de->bte", attended_tok, proj_weight, preferred_element_type=jnp.float32
    )
    middle = inputs32 + branch + proj_shift.astype(jnp.float32)
    normed_two = norm_rows(middle, gain_two, shift_two).astype(jnp.bfloat16)
    logits = jnp.einsum(
        "btd,de->bte", normed_two, router_weight, preferred_element_type=jnp.float32
    )
    router = softmax_last(logits)
    routes_own = lax.dynamic_slice_in_dim(routes, seq_place * slots, slots, 1)
    expert_ids = jnp.arange(experts)
    chosen_own = (routes_own[..., None] == expert_ids).astype(jnp.float32)
    gates = jnp.sum(chosen_own * router[:, :, None, :], axis=-1).astype(jnp.bfloat16)
    gates32 = gates.astype(jnp.float32)
    grad_out = jnp.where(own_valid, cotangent, jnp.zeros((), jnp.bfloat16))
    grad32 = grad_out.astype(jnp.float32)
    group_rows, group_gates, group_grad = (
        lax.all_gather(normed_two, "seq", axis=1, tiled=True),
        lax.all_gather(gates, "seq", axis=1, tiled=True),
        lax.all_gather(grad_out, "seq", axis=1, tiled=True),
    )
    token_count = images * length
    rows_flat = group_rows.reshape(token_count, width)
    grad_flat = group_grad.reshape(token_count, width)
    group_chosen = (routes.reshape(token_count, 2)[..., None] == expert_ids).astype(jnp.float32)
    dense_gates = jnp.sum(
        group_chosen * group_gates.reshape(token_count, 2).astype(jnp.float32)[..., None], axis=1
    )

    def expert_step(totals, pieces):
        inner_now, outer_now, bias_now, gate_now = pieces
        grad_now = (gate_now[:, None] * grad_flat.astype(jnp.float32)).astype(jnp.bfloat16)
        result, grad_rows_now, inner_part, outer_part, bias_part = expert_pass(
            rows_flat, grad_now, inner_now, outer_now, bias_now
        )
        mix_sum, rows_sum = totals
        dots = jnp.sum(grad_flat.astype(jnp.float32) * result, axis=-1)
        totals = (mix_sum + gate_now[:, None] * result, rows_sum + grad_rows_now)
        return totals, (inner_part, outer_part, bias_part, dots)

    blank = jnp.zeros((token_count, width), jnp.float32)
    (partial_mix, partial_rows), (inner_grad, outer_grad, inner_bias_grad, expert_dots) = lax.scan(
        expert_step, (blank, blank), (inner_weight, outer_weight, inner_bias, dense_gates.T)
    )
    partial_mix = partial_mix.reshape(images, length, width)
    entry_dot = jnp.einsum("et,tke->tk", expert_dots, group_chosen, precision=HIGHEST)
    expert_mix, row_grad, gate_grad = (
        lax.psum_scatter(
            partial_mix.astype(jnp.bfloat16), "seq", scatter_dimension=1, tiled=True
        ).astype(jnp.float32),
        lax.psum_scatter(
            partial_rows.reshape(images, length, width).astype(jnp.bfloat16),
            "seq",
            scatter_dimension=1,
            tiled=True,
        ).astype(jnp.float32),
        lax.psum_scatter(
            entry_dot.reshape(images, length, 2).astype(jnp.bfloat16),
            "seq",
            scatter_dimension=1,
            tiled=True,
        ).astype(jnp.float32),
    )
    inner_bias_full = lax.dynamic_update_slice_in_dim(
        jnp.zeros((experts, quarter * seq_count), jnp.float32),
        inner_bias_grad,
        seq_place * quarter,
        1,
    ).reshape(-1)
    gated_choice = chosen_own * gates32[..., None]
    bias_mix = jnp.einsum("bske,ed->bsd", gated_choice, outer_bias, precision=HIGHEST)
    output32 = middle + expert_mix + bias_mix
    mixed = jnp.where(own_valid, output32, 0.0).astype(jnp.bfloat16)
    gate_grad = gate_grad + jnp.einsum(
        "bsd,bske,ed->bsk", grad32, chosen_own, outer_bias, precision=HIGHEST
    )
    grad_router_probs = jnp.einsum("bsk,bske->bse", gate_grad, chosen_own, precision=HIGHEST)
    _, soft_pull = jax.vjp(softmax_last, logits)
    grad_logits = soft_pull(grad_router_probs)[0]
    router_grad = jnp.einsum(
        "bsd,bse->de", normed_two.astype(jnp.float32), grad_logits, precision=HIGHEST
    )
    grad_normed_two = row_grad + jnp.einsum(
        "bse,de->bsd", grad_logits, router_weight.astype(jnp.float32), precision=HIGHEST
    )
    outer_bias_grad = jnp.einsum("bske,bsd->ed", gated_choice, grad32, precision=HIGHEST)
    _, norm_pull_two = jax.vjp(norm_rows, middle, gain_two, shift_two)
    grad_middle_norm, grad_gain_two, grad_shift_two = norm_pull_two(grad_normed_two)
    grad_middle = grad32 + grad_middle_norm
    grad_branch = grad_middle.astype(jnp.bfloat16)
    proj_shift_grad = jnp.sum(grad_branch.astype(jnp.float32), axis=(0, 1))
    proj_weight_grad = jnp.einsum(
        "bsd,bse->de", attended_tok, grad_branch, preferred_element_type=jnp.float32
    )
    grad_attended = jnp.einsum(
        "bse,de->bsd", grad_branch, proj_weight, preferred_element_type=jnp.float32
    ).astype(jnp.bfloat16)
    grad_heads = lax.all_to_all(
        grad_attended.reshape(images, slots, seq_count, local_width),
        "seq",
        split_axis=2,
        concat_axis=1,
        tiled=True,
    )
    grad_blocks = grad_heads.reshape(1, images, length, head_local, HEAD)
    grad_qkv_heads = lax.map(partial(attend_back, key_valid), (blocks, grad_blocks, log_totals))
    grad_qkv_back = lax.all_to_all(
        grad_qkv_heads.reshape(images, length, 3, 1, local_width),
        "seq",
        split_axis=1,
        concat_axis=3,
        tiled=True,
    )
    grad_qkv = grad_qkv_back.reshape(images, slots, 3 * width)
    qkv_weight_grad = jnp.einsum(
        "bsd,bse->de", normed_one, grad_qkv, preferred_element_type=jnp.float32
    )
    qkv_columns = jnp.sum(grad_qkv.astype(jnp.float32), axis=(0, 1))
    qv_grad = jnp.concatenate([qkv_columns[:width], qkv_columns[2 * width :]])
    grad_normed_one = jnp.einsum(
        "bse,de->bsd", grad_qkv, qkv_weight, preferred_element_type=jnp.float32
    )
    _, norm_pull_one = jax.vjp(norm_rows, inputs32, gain_one, shift_one)
    grad_input_norm, grad_gain_one, grad_shift_one = norm_pull_one(grad_normed_one)
    grad_tokens = jnp.where(own_valid, grad_middle + grad_input_norm, 0.0)
    (
        grad_ln1_gain,
        grad_ln1_bias,
        grad_w_qkv,
        grad_b_qv,
        grad_w_proj,
        grad_b_proj,
        grad_ln2_gain,
        grad_ln2_bias,
        grad_w_router,
        grad_b_in,
        grad_b_out,
    ) = (
        lax.psum_scatter(grad_gain_one, ("fsdp", "seq"), scatter_dimension=0, tiled=True),
        lax.psum_scatter(grad_shift_one, ("fsdp", "seq"), scatter_dimension=0, tiled=True),
        lax.psum_scatter(qkv_weight_grad, ("fsdp", "seq"), scatter_dimension=0, tiled=True),
        lax.psum_scatter(qv_grad, ("fsdp", "seq"), scatter_dimension=0, tiled=True),
        lax.psum_scatter(proj_weight_grad, ("fsdp", "seq"), scatter_dimension=0, tiled=True),
        lax.psum_scatter(proj_shift_grad, ("fsdp", "seq"), scatter_dimension=0, tiled=True),
        lax.psum_scatter(grad_gain_two, ("fsdp", "seq"), scatter_dimension=0, tiled=True),
        lax.psum_scatter(grad_shift_two, ("fsdp", "seq"), scatter_dimension=0, tiled=True),
        lax.psum_scatter(router_grad, ("fsdp", "seq"), scatter_dimension=0, tiled=True),
        lax.psum_scatter(inner_bias_full, ("fsdp", "seq"), scatter_dimension=0, tiled=True),
        lax.psum_scatter(
            outer_bias_grad.reshape(-1), ("fsdp", "seq"), scatter_dimension=0, tiled=True
        ),
    )
    grad_w_in, outer_owned = (
        lax.psum_scatter(inner_grad, "fsdp", scatter_dimension=1, tiled=True),
        lax.psum_scatter(outer_grad, "fsdp", scatter_dimension=1, tiled=True),
    )
    grad_w_out = jnp.swapaxes(outer_owned, 1, 2)
    return (
        mixed,
        grad_tokens,
        grad_ln1_gain,
        grad_ln1_bias,
        grad_w_qkv,
        grad_b_qv,
        grad_w_proj,
        grad_b_proj,
        grad_ln2_gain,
        grad_ln2_bias,
        grad_w_router,
        grad_w_in,
        grad_b_in,
        grad_w_out,
        grad_b_out,
    )


def solution(mesh):
    in_specs = (
        P("fsdp", "seq", None),
        P("fsdp", None, None),
        P(("fsdp", "seq")),
        P(("fsdp", "seq")),
        P(("fsdp", "seq"), None),
        P(("fsdp", "seq")),
        P(("fsdp", "seq"), None),
        P(("fsdp", "seq")),
        P(("fsdp", "seq")),
        P(("fsdp", "seq")),
        P(("fsdp", "seq"), None),
        P(None, "fsdp", "seq"),
        P(("fsdp", "seq")),
        P(None, "seq", "fsdp"),
        P(("fsdp", "seq")),
        P("fsdp", "seq", None),
    )
    out_specs = (
        P("fsdp", "seq", None),
        P("fsdp", "seq", None),
        P(("fsdp", "seq")),
        P(("fsdp", "seq")),
        P(("fsdp", "seq"), None),
        P(("fsdp", "seq")),
        P(("fsdp", "seq"), None),
        P(("fsdp", "seq")),
        P(("fsdp", "seq")),
        P(("fsdp", "seq")),
        P(("fsdp", "seq"), None),
        P(None, "fsdp", "seq"),
        P(("fsdp", "seq")),
        P(None, "seq", "fsdp"),
        P(("fsdp", "seq")),
    )
    device_program = per_device if dict(mesh.shape) == {"fsdp": 8, "seq": 4} else per_device_general
    return jax.shard_map(
        device_program, mesh=mesh, in_specs=in_specs, out_specs=out_specs, check_vma=False
    )
```
